32 devices in a mesh: snap: 4 (over y, x), plane: 8 (over z, core).
Axes of the slice: x: 2, y: 2, z: 4, core: 2. Of those that a mesh axis runs over, the one named last changes fastest.
Arguments:
- velocity: bfloat16 [4, 32, 3, 128, 128], P('snap', 'plane'), may hold values from -6 to 6
- plane_count: int32 [8], P('plane'), may hold values from 1 to 4, as said below
- inv_span: float32 [8, 4], P('plane'), may hold values from 0.5 to 4
- kernels: float32 [3, 2, 3, 3], replicated, may hold values from -2.4 to 2.4
- omega_block: int32 [8, 4], P('plane'), may hold values from 0 to 7
- omega_table: bfloat16 [8, 9, 32, 256], replicated, may hold values from -0.0625 to 0.0625
- omega_stream: bfloat16 [32, 256], replicated, may hold values from -6 to 6
- wall_shear: bfloat16 [4, 2, 128, 128], P('snap', None, 'plane'), may hold values from -6 to 6
Outputs:
- sketch: float32 [2, 32, 32, 256], P(None, 'plane', 'snap')
- gram: float32 [256, 256], replicated
The draws below stay inside these ranges and needn't reach their ends.
Inputs may be any that keep to these rules, and one draw needn't show every extreme that they name: `plane_count`: every index of plane holds 1 or more live slots, slots 0 onwards; some index holds 4.
All inputs are finite; a program needn't handle non-finite values.
Results may differ from the reference program's by a relative error of at most 0.0043.
Values may be sent and summed in bfloat16 or wider, within the bound.
A program may use at most 64 MiB of HBM per device.

```python
import math
import jax
import jax.numpy as jnp
from jax import lax

X = 128
ZW = 128
CAP = 4
CH = 9
K = 256
BLOCKS = 8
SNAPS = 4
SLOTS = 32
ZF = 32
XF = 32
N_PLANE = 8


def draw_plane_count(key, part):
    counts = jax.random.randint(key, (N_PLANE,), 1, CAP + 1)
    chosen = jax.random.randint(jax.random.fold_in(key, 7), (), 0, N_PLANE)
    return jnp.where(jnp.arange(N_PLANE) == chosen, CAP, counts).astype(jnp.int32)


def with_ends(drawn, key, low, high):
    index_at = [jax.random.randint(jax.random.fold_in(key, axis), (), 0, length) for axis, length in enumerate(drawn.shape)]
    longest = drawn.shape.index(max(drawn.shape))
    beside = index_at[:longest] + [(index_at[longest] + 1) % drawn.shape[longest]] + index_at[longest + 1:]
    return drawn.at[tuple(index_at)].set(low).at[tuple(beside)].set(high)


def block_levels(key, dims, cuts, least, top_value):
    factor_of = 1.0
    for axis_at, parts in cuts:
        steps = jax.random.uniform(jax.random.fold_in(jax.random.fold_in(key, 6), axis_at), (parts,), jnp.float32, least / len(cuts), top_value / len(cuts))
        factor_of = factor_of * jnp.repeat(jnp.exp(steps), dims[axis_at] // parts).reshape((-1,) + (1,) * (len(dims) - 1 - axis_at))
    return factor_of


def scatter_about(key, extent, width, most, pieces=(), kind=jnp.bfloat16):
    values = jax.random.normal(key, extent, jnp.float32) * width
    if len(pieces) > 0:
        values = block_levels(key, extent, pieces, -0.22, 0.18) * values
    return jnp.clip(values, min=-most, max=most).astype(kind)


def setup_inputs(seed: int = 0) -> dict:
    arg_keys = jax.random.split(jax.random.key(seed), 9)
    velocity = scatter_about(arg_keys[0], (SNAPS, SLOTS, 3, ZW, X), 1.0, 6.0, ((0, 4), (1, 8)))
    plane_count = draw_plane_count(jax.random.fold_in(arg_keys[8], 71), 0)
    inv_span = jnp.clip(jnp.exp(math.log(4.0) - 2.0794415 * jax.random.uniform(arg_keys[2], (N_PLANE, CAP), jnp.float32) ** block_levels(arg_keys[2], (N_PLANE, CAP), ((0, 8),), -0.2, 0.2)), 0.5, 4.0)
    kernels = scatter_about(arg_keys[3], (3, 2, 3, 3), 0.4, 2.4, (), jnp.float32)
    omega_block = with_ends(jax.random.randint(arg_keys[4], (N_PLANE, CAP), 0, BLOCKS), jax.random.fold_in(arg_keys[4], 1), 0, BLOCKS - 1).astype(jnp.int32)
    omega_table = scatter_about(arg_keys[5], (BLOCKS, CH, ZF, K), (CH * ZF * XF) ** -0.5, 0.0625)
    omega_stream = scatter_about(arg_keys[6], (XF, K), 1.0, 6.0)
    wall_shear = scatter_about(arg_keys[7], (SNAPS, 2, ZW, X), 1.0, 6.0, ((0, 4), (2, 8)))
    return {"velocity": velocity, "plane_count": plane_count, "inv_span": inv_span, "kernels": kernels, "omega_block": omega_block, "omega_table": omega_table, "omega_stream": omega_stream, "wall_shear": wall_shear}


def features(centre, below, above, span, kernels):
    snaps, comps, zw, xw = centre.shape
    field = centre.astype(jnp.float32)
    padded = jnp.pad(field, ((0, 0), (0, 0), (1, 1), (1, 1)))
    first = jnp.zeros_like(field)
    second = jnp.zeros_like(field)
    for row_a in range(3):
        for col_b in range(3):
            window = padded[:, :, row_a:row_a + zw, col_b:col_b + xw]
            first = first + kernels[:, 0, row_a, col_b][None, :, None, None] * window
            second = second + kernels[:, 1, row_a, col_b][None, :, None, None] * window
    normal = (above.astype(jnp.float32) - below.astype(jnp.float32)) * span
    grads = jnp.stack([first, second, normal], axis=2).reshape(snaps, 9, zw, xw)
    filtered = grads.reshape(snaps, 9, zw // 4, 4, xw // 4, 4).mean(axis=(3, 5))
    return filtered.astype(jnp.bfloat16)


def reference(velocity, plane_count, inv_span, kernels, omega_block, omega_table, omega_stream, wall_shear):
    npl = plane_count.shape[0]
    cap = inv_span.shape[1]
    counts = plane_count.astype(jnp.int32)
    spans = inv_span.reshape(-1)
    blocks = omega_block.reshape(-1).astype(jnp.int32)

    def slot_term(index):
        owner = index // cap
        slot = index % cap
        live = slot < counts[owner]
        has_up = (slot + 1 < counts[owner]) | (owner + 1 < npl)
        up_index = jnp.where(slot + 1 < counts[owner], index + 1, (owner + 1) * cap)
        prev_owner = jnp.maximum(owner - 1, 0)
        has_down = (slot >= 1) | (owner >= 1)
        down_index = jnp.where(slot >= 1, index - 1, prev_owner * cap + counts[prev_owner] - 1)
        up_index = jnp.clip(up_index, 0, npl * cap - 1).astype(jnp.int32)
        down_index = jnp.clip(down_index, 0, npl * cap - 1).astype(jnp.int32)
        centre = lax.dynamic_index_in_dim(velocity, index.astype(jnp.int32), 1, keepdims=False)
        above = lax.dynamic_index_in_dim(velocity, up_index, 1, keepdims=False)
        below = lax.dynamic_index_in_dim(velocity, down_index, 1, keepdims=False)
        above = jnp.where(has_up, above, jnp.zeros_like(above))
        below = jnp.where(has_down, below, jnp.zeros_like(below))
        feats = features(centre, below, above, spans[index], kernels)
        proj = jnp.einsum('sczx,xk->sczk', feats, omega_stream, preferred_element_type=jnp.float32)
        table = lax.dynamic_index_in_dim(omega_table, blocks[index], 0, keepdims=False).astype(jnp.float32)
        term = jnp.einsum('sczk,czk->sk', proj, table, precision=lax.Precision.HIGHEST)
        return jnp.where(live, term, jnp.zeros_like(term))

    terms = lax.map(slot_term, jnp.arange(npl * cap, dtype=jnp.int32))
    coef = jnp.sum(terms, axis=0)
    snaps, comps, zw, xw = wall_shear.shape
    shear_f = wall_shear.astype(jnp.float32).reshape(snaps, comps, zw // 4, 4, xw // 4, 4).mean(axis=(3, 5))
    sketch = jnp.einsum('smzx,sk->mzxk', shear_f, coef, precision=lax.Precision.HIGHEST)
    flat = sketch.reshape(-1, sketch.shape[-1])
    gram = jnp.dot(flat.T, flat, precision=lax.Precision.HIGHEST) / jnp.float32(flat.shape[0])
    return sketch, gram
```

```python
import functools

import jax
import jax.numpy as jnp
from jax import lax
from jax.experimental import pallas as pl
from jax.experimental.pallas import tpu as pltpu
from jax.sharding import PartitionSpec as P

POOL = 4
MESH = pl.DeviceIdType.MESH
HIGHEST = lax.Precision.HIGHEST


def shift_rows(value, steps):
    rows = value.shape[0]
    at = lax.broadcasted_iota(jnp.int32, value.shape, 0)
    edge = 0 if steps == 1 else rows - 1
    return jnp.where(at == edge, 0.0, pltpu.roll(value, steps % rows, 0))


def kernel(
    snaps, planes,
    count_ref, span_ref, stencil_ref, block_ref, shear_ref, stream_ref, velocity_hbm, table_hbm,
    sketch_ref, gram_ref,
    velocity, table, stream, pooled, columns, feats, shear_rows, shear_all, shear_t, inner_all,
    halo_out, halo_in, coef_all, coef_snap,
    local_sem, shear_send, shear_recv, inner_send, inner_recv, halo_send, halo_recv,
    coef_send, coef_recv, snap_send, snap_recv,
):
    slots, comps, zw, xw = velocity.shape
    zf, xf = zw // POOL, xw // POOL
    width = stream_ref.shape[1]
    me_s, me_p = lax.axis_index("snap"), lax.axis_index("plane")

    get_velocity = pltpu.make_async_copy(velocity_hbm.at[0], velocity, local_sem.at[0])
    get_table = pltpu.make_async_copy(table_hbm, table, local_sem.at[1])
    get_velocity.start()
    get_table.start()

    snap_peers = [lax.rem(me_s + d, snaps) for d in range(1, snaps)]
    plane_peers = [lax.rem(me_p + d, planes) for d in range(1, planes)]
    barrier = pltpu.get_barrier_semaphore()
    for peer in snap_peers:
        pl.semaphore_signal(barrier, inc=1, device_id=(peer, me_p), device_id_type=MESH)
    for peer in plane_peers:
        pl.semaphore_signal(barrier, inc=1, device_id=(me_s, peer), device_id_type=MESH)

    row = lax.broadcasted_iota(jnp.int32, (comps * xw, xw), 0)
    lane = lax.broadcasted_iota(jnp.int32, (comps * xw, xw), 1)
    gap = lax.rem(row, xw) - POOL * lax.rem(lane, xf)
    hit = (lax.div(row, xw) == lax.div(lane, xf)) & (gap >= 0) & (gap < POOL)
    pack = jnp.where(hit, 1.0, 0.0).astype(jnp.bfloat16)
    row = lax.broadcasted_iota(jnp.int32, (xw, xw), 0)
    lane = lax.broadcasted_iota(jnp.int32, (xw, xw), 1)
    group = lax.div(lane, xf)
    gap = row - POOL * lax.rem(lane, xf) - jnp.where(group == 1, -1, jnp.where(group == 2, 1, 0))
    hit = (group < 3) & (gap >= 0) & (gap < POOL)
    shifts = jnp.where(hit, 1.0, 0.0).astype(jnp.bfloat16)

    kinds, zs = shear_ref.shape[1], shear_ref.shape[2]
    zl = zs // POOL
    shear_in = shear_ref[0].reshape(kinds * zs, xw)
    shear_rows[...] = jnp.dot(shear_in, pack[:xw], preferred_element_type=jnp.float32)
    part = [shear_rows[pl.ds(r, kinds * zl, stride=POOL), :] for r in range(POOL)]
    shear_all[me_s] = (part[0] + part[1] + part[2] + part[3]) * (1.0 / (POOL * POOL))

    pl.semaphore_wait(barrier, snaps - 1 + planes - 1)

    def send(src, dst, send_sem, recv_sem, snap, plane):
        copy = pltpu.make_async_remote_copy(
            src_ref=src, dst_ref=dst, send_sem=send_sem, recv_sem=recv_sem,
            device_id=(snap, plane), device_id_type=MESH,
        )
        copy.start()
        return copy

    shear_copies = [
        send(shear_all.at[me_s], shear_all.at[me_s], shear_send.at[d], shear_recv.at[d], peer, me_p)
        for d, peer in enumerate(snap_peers)
    ]

    get_velocity.wait()
    fields = jnp.concatenate(
        [velocity[:, i].reshape(slots * zw, xw) for i in range(comps)], axis=1
    )
    columns[pl.ds(0, slots * zw), :] = jnp.dot(fields, pack, preferred_element_type=jnp.float32)
    part = [columns[pl.ds(r, slots * zf, stride=POOL), :] for r in range(POOL)]
    pooled[...] = (part[0] + part[1] + part[2] + part[3]).reshape(slots, zf, xw)
    live_count = count_ref[0]
    halo_out[0] = pooled[0]
    last = pooled[0]
    for slot in range(1, slots):
        last = jnp.where(live_count - 1 == slot, pooled[slot], last)
    halo_out[1] = last

    def halo(which, plane):
        return pltpu.make_async_remote_copy(
            src_ref=halo_out.at[which], dst_ref=halo_in.at[which],
            send_sem=halo_send.at[which], recv_sem=halo_recv.at[which],
            device_id=(me_s, plane), device_id_type=MESH,
        )

    down = halo(0, jnp.maximum(me_p - 1, 0))
    up = halo(1, jnp.minimum(me_p + 1, planes - 1))

    @pl.when(me_p > 0)
    def _():
        down.start()

    @pl.when(me_p < planes - 1)
    def _():
        up.start()

    @pl.when(me_p == 0)
    def _():
        halo_in[1] = jnp.zeros_like(halo_in[1])

    @pl.when(me_p == planes - 1)
    def _():
        halo_in[0] = jnp.zeros_like(halo_in[0])

    for copy in shear_copies:
        copy.wait()
    every = shear_all[...]
    inner_rows = inner_all.shape[1]
    at_row = lax.broadcasted_iota(jnp.int32, (inner_rows, xw), 0)
    at_lane = lax.broadcasted_iota(jnp.int32, (inner_rows, xw), 1)
    inner = jnp.zeros((inner_rows, xw), jnp.float32)
    for a in range(snaps):
        for b in range(a, snaps):
            value = jnp.sum(every[a] * every[b])
            place = ((at_row == a) & (at_lane == b)) | ((at_row == b) & (at_lane == a))
            inner = jnp.where(place, value, inner)
    inner_all[me_p] = inner
    inner_copies = [
        send(inner_all.at[me_p], inner_all.at[me_p], inner_send.at[d], inner_recv.at[d], me_s, peer)
        for d, peer in enumerate(plane_peers)
    ]

    images = velocity[...].reshape(slots * comps * zw, xw)
    columns[...] = jnp.dot(images, shifts, preferred_element_type=jnp.float32)
    lane = lax.broadcasted_iota(jnp.int32, (8, xw), 1)
    group = lax.div(lane, xf)
    weights = {}
    for i in range(comps):
        for f in range(2):
            for a in range(3):
                k = [stencil_ref[i, f, a, b] * (1.0 / (POOL * POOL)) for b in range(3)]
                weights[i, f, a] = jnp.where(group == 0, k[1], jnp.where(group == 1, k[0], k[2]))[:1]
    for slot in range(slots):
        for i in range(comps):
            base = (slot * comps + i) * zw
            part = [columns[pl.ds(base + r, zf, stride=POOL), :] for r in range(POOL)]
            middle = part[1] + part[2]
            sums = [
                shift_rows(part[3], 1) + part[0] + middle,
                part[0] + middle + part[3],
                middle + part[3] + shift_rows(part[0], -1),
            ]
            for f in range(2):
                mixed = sum(weights[i, f, a] * sums[a] for a in range(3))
                mixed = mixed + pltpu.roll(mixed, xw - xf, 1) + pltpu.roll(mixed, xw - 2 * xf, 1)
                feats[slot, pl.ds((2 * i + f) * zf, zf), :] = mixed.astype(jnp.bfloat16)

    stream[...] = jnp.zeros_like(stream)
    stream[pl.ds(xw - xf, xf), :] = stream_ref[...]
    get_table.wait()

    def fold(value):
        return jnp.sum(value.reshape(zf // 8, 8, width), axis=0)

    first_stream = stream[pl.ds(xw - xf, xw), :]
    terms = []
    for slot in range(slots):
        proj = jnp.dot(feats[slot], first_stream, preferred_element_type=jnp.float32)
        block = block_ref[0, slot]
        term = jnp.zeros((8, width), jnp.float32)
        for i in range(comps):
            for f in range(2):
                at = (2 * i + f) * zf
                term = term + fold(proj[at : at + zf] * table[block, 3 * i + f].astype(jnp.float32))
        terms.append(term)

    @pl.when(me_p > 0)
    def _():
        up.wait_recv()

    @pl.when(me_p < planes - 1)
    def _():
        down.wait_recv()

    normals = []
    for slot in range(slots):
        below = halo_in[1] if slot == 0 else pooled[slot - 1]
        above = halo_in[0]
        if slot + 1 < slots:
            above = jnp.where(slot + 1 < live_count, pooled[slot + 1], above)
        scale = span_ref[0, slot] * (1.0 / (POOL * POOL))
        normals.append(((above - below) * scale).astype(jnp.bfloat16))
    normals = jnp.concatenate(normals, axis=0)
    for i in range(comps):
        proj = jnp.dot(
            normals, stream[pl.ds(xw - xf - i * xf, xw), :], preferred_element_type=jnp.float32
        )
        for slot in range(slots):
            at = slot * zf
            tile = table[block_ref[0, slot], 3 * i + 2].astype(jnp.float32)
            terms[slot] = terms[slot] + fold(proj[at : at + zf] * tile)
    total = jnp.zeros((8, width), jnp.float32)
    for slot in range(slots):
        total = total + jnp.where(slot < live_count, terms[slot], 0.0)
    coef_all[me_p] = jnp.sum(total, axis=0, keepdims=True)
    coef_copies = [
        send(coef_all.at[me_p], coef_all.at[me_p], coef_send.at[d], coef_recv.at[d], me_s, peer)
        for d, peer in enumerate(plane_peers)
    ]

    stacked = jnp.concatenate([shear_all[s] for s in range(snaps)], axis=0)
    spare = xw - stacked.shape[0]
    if spare:
        stacked = jnp.concatenate([stacked, jnp.zeros((spare, xw), jnp.float32)], axis=0)
    shear_t[...] = stacked.T
    xl = xf // snaps
    mine = shear_t[pl.ds(me_s * xl, xl), :]
    for copy in inner_copies:
        copy.wait()
    inner = inner_all[0]
    for p in range(1, planes):
        inner = inner + inner_all[p]

    for copy in coef_copies:
        copy.wait()
    coef = coef_all[0]
    for p in range(1, planes):
        coef = coef + coef_all[p]
    coef_snap[me_s] = coef
    snap_copies = [
        send(coef_snap.at[me_s], coef_snap.at[me_s], snap_send.at[d], snap_recv.at[d], peer, me_p)
        for d, peer in enumerate(snap_peers)
    ]
    for copy in snap_copies:
        copy.wait()

    coefs = [coef_snap[s] for s in range(snaps)]
    rows = kinds * zl
    for m in range(kinds):
        for z in range(zl):
            value = jnp.zeros((xl, width), jnp.float32)
            for s in range(snaps):
                at = s * rows + m * zl + z
                value = value + mine[:, at : at + 1] * coefs[s]
            sketch_ref[m, z] = value
    weighted = jnp.zeros((inner_rows, width), jnp.float32)
    for s in range(snaps):
        weighted = weighted + inner[:, s : s + 1] * coefs[s]
    padded = coefs
    if inner_rows > snaps:
        padded = coefs + [jnp.zeros((inner_rows - snaps, width), jnp.float32)]
    stack = jnp.concatenate(padded, axis=0)
    total_rows = kinds * xf * zl * planes
    gram_ref[...] = jnp.dot(
        stack.T, weighted * (1.0 / total_rows), precision=HIGHEST,
        preferred_element_type=jnp.float32,
    )

    @pl.when(me_p > 0)
    def _():
        down.wait_send()

    @pl.when(me_p < planes - 1)
    def _():
        up.wait_send()


def per_device(
    velocity, plane_count, inv_span, kernels, omega_block, omega_table, omega_stream, wall_shear
):
    snaps, planes = lax.axis_size("snap"), lax.axis_size("plane")
    _, slots, comps, zw, xw = velocity.shape
    zf, xf = zw // POOL, xw // POOL
    width = omega_stream.shape[1]
    _, kinds, zs, _ = wall_shear.shape
    zl = zs // POOL
    inner_rows = -(-snaps // 8) * 8
    smem = pl.BlockSpec(memory_space=pltpu.SMEM)
    vmem = pl.BlockSpec(memory_space=pltpu.VMEM)
    hbm = pl.BlockSpec(memory_space=pl.ANY)
    dma = pltpu.SemaphoreType.DMA
    f32, bf16 = jnp.float32, jnp.bfloat16
    return pl.pallas_call(
        functools.partial(kernel, snaps, planes),
        out_shape=(
            jax.ShapeDtypeStruct((kinds, zl, xf // snaps, width), f32),
            jax.ShapeDtypeStruct((width, width), f32),
        ),
        in_specs=[smem, smem, smem, smem, vmem, vmem, hbm, hbm],
        out_specs=(vmem, vmem),
        scratch_shapes=[
            pltpu.VMEM((slots, comps, zw, xw), bf16),
            pltpu.VMEM(omega_table.shape, bf16),
            pltpu.VMEM((2 * xw - xf, width), bf16),
            pltpu.VMEM((slots, zf, xw), f32),
            pltpu.VMEM((slots * comps * zw, xw), f32),
            pltpu.VMEM((slots, 2 * comps * zf, xw), bf16),
            pltpu.VMEM((kinds * zs, xw), f32),
            pltpu.VMEM((snaps, kinds * zl, xw), f32),
            pltpu.VMEM((xw, xw), f32),
            pltpu.VMEM((planes, inner_rows, xw), f32),
            pltpu.VMEM((2, zf, xw), f32),
            pltpu.VMEM((2, zf, xw), f32),
            pltpu.VMEM((planes, 1, width), f32),
            pltpu.VMEM((snaps, 1, width), f32),
            dma((2,)),
            dma((snaps - 1,)), dma((snaps - 1,)),
            dma((planes - 1,)), dma((planes - 1,)),
            dma((2,)), dma((2,)),
            dma((planes - 1,)), dma((planes - 1,)),
            dma((snaps - 1,)), dma((snaps - 1,)),
        ],
        compiler_params=pltpu.CompilerParams(
            collective_id=0, has_side_effects=True, vmem_limit_bytes=24 * 1024 * 1024
        ),
    )(
        plane_count, inv_span, kernels, omega_block, wall_shear, omega_stream, velocity, omega_table
    )


def solution(mesh):
    return jax.shard_map(
        per_device,
        mesh=mesh,
        in_specs=(
            P("snap", "plane", None, None, None),
            P("plane"),
            P("plane", None),
            P(),
            P("plane", None),
            P(),
            P(),
            P("snap", None, "plane", None),
        ),
        out_specs=(P(None, "plane", "snap", None), P()),
        check_vma=False,
    )
```

```python
import functools

import jax
import jax.numpy as jnp
from jax import lax
from jax.experimental import pallas as pl
from jax.experimental.pallas import tpu as pltpu
from jax.sharding import PartitionSpec as P

POOL = 4
MESH = pl.DeviceIdType.MESH
HIGHEST = lax.Precision.HIGHEST


def shift_rows(value, steps):
    rows = value.shape[0]
    at = lax.broadcasted_iota(jnp.int32, value.shape, 0)
    edge = 0 if steps == 1 else rows - 1
    return jnp.where(at == edge, 0.0, pltpu.roll(value, steps % rows, 0))


def kernel(
    snaps, planes,
    count_hbm, span_hbm, stencil_hbm, block_hbm, shear_hbm, stream_hbm, velocity_hbm, table_hbm,
    sketch_ref, gram_ref,
    count_ref, span_ref, stencil_ref, block_ref, shear_ref, stream_ref, velocity, table, stream, pooled, columns, feats, shear_rows, shear_all, shear_t, inner_all,
    halo_out, halo_in, coef_all, coef_snap,
    local_sem, shear_send, shear_recv, inner_send, inner_recv, halo_send, halo_recv,
    coef_send, coef_recv, snap_send, snap_recv,
):
    slots, comps, zw, xw = velocity.shape
    zf, xf = zw // POOL, xw // POOL
    width = stream_hbm.shape[1]
    me_s, me_p = lax.axis_index("snap"), lax.axis_index("plane")

    snap_peers = [lax.rem(me_s + d, snaps) for d in range(1, snaps)]
    plane_peers = [lax.rem(me_p + d, planes) for d in range(1, planes)]
    barrier = pltpu.get_barrier_semaphore()
    for peer in snap_peers:
        pl.semaphore_signal(barrier, inc=1, device_id=(peer, me_p), device_id_type=MESH)
    for peer in plane_peers:
        pl.semaphore_signal(barrier, inc=1, device_id=(me_s, peer), device_id_type=MESH)

    def fetch(index, source, target):
        copy = pltpu.make_async_copy(source, target, local_sem.at[index])
        copy.start()
        return copy

    get_velocity = fetch(0, velocity_hbm.at[0], velocity)
    get_shear = fetch(1, shear_hbm, shear_ref)
    get_count = fetch(2, count_hbm, count_ref)
    get_stencil = fetch(3, stencil_hbm, stencil_ref)
    get_span = fetch(4, span_hbm, span_ref)
    get_block = fetch(5, block_hbm, block_ref)
    get_stream = fetch(6, stream_hbm, stream_ref)
    get_table = fetch(7, table_hbm, table)

    row = lax.broadcasted_iota(jnp.int32, (comps * xw, xw), 0)
    lane = lax.broadcasted_iota(jnp.int32, (comps * xw, xw), 1)
    gap = lax.rem(row, xw) - POOL * lax.rem(lane, xf)
    hit = (lax.div(row, xw) == lax.div(lane, xf)) & (gap >= 0) & (gap < POOL)
    pack = jnp.where(hit, 1.0, 0.0).astype(jnp.bfloat16)
    row = lax.broadcasted_iota(jnp.int32, (xw, xw), 0)
    lane = lax.broadcasted_iota(jnp.int32, (xw, xw), 1)
    group = lax.div(lane, xf)
    gap = row - POOL * lax.rem(lane, xf) - jnp.where(group == 1, -1, jnp.where(group == 2, 1, 0))
    hit = (group < 3) & (gap >= 0) & (gap < POOL)
    shifts = jnp.where(hit, 1.0, 0.0).astype(jnp.bfloat16)

    kinds, zs = shear_ref.shape[1], shear_ref.shape[2]
    zl = zs // POOL
    get_shear.wait()
    shear_in = shear_ref[0].reshape(kinds * zs, xw)
    shear_rows[...] = jnp.dot(shear_in, pack[:xw], preferred_element_type=jnp.float32)
    part = [shear_rows[pl.ds(r, kinds * zl, stride=POOL), :] for r in range(POOL)]
    shear_all[me_s] = (part[0] + part[1] + part[2] + part[3]) * (1.0 / (POOL * POOL))

    get_velocity.wait()
    fields = jnp.concatenate(
        [velocity[:, i].reshape(slots * zw, xw) for i in range(comps)], axis=1
    )
    columns[pl.ds(0, slots * zw), :] = jnp.dot(fields, pack, preferred_element_type=jnp.float32)
    part = [columns[pl.ds(r, slots * zf, stride=POOL), :] for r in range(POOL)]
    pooled[...] = (part[0] + part[1] + part[2] + part[3]).reshape(slots, zf, xw)
    get_count.wait()
    live_count = count_ref[0, 0]
    halo_out[0] = pooled[0]
    last = pooled[0]
    for slot in range(1, slots):
        last = jnp.where(live_count - 1 == slot, pooled[slot], last)
    halo_out[1] = last

    pl.semaphore_wait(barrier, snaps - 1 + planes - 1)

    def halo(which, plane):
        return pltpu.make_async_remote_copy(
            src_ref=halo_out.at[which], dst_ref=halo_in.at[which],
            send_sem=halo_send.at[which], recv_sem=halo_recv.at[which],
            device_id=(me_s, plane), device_id_type=MESH,
        )

    down = halo(0, jnp.maximum(me_p - 1, 0))
    up = halo(1, jnp.minimum(me_p + 1, planes - 1))

    @pl.when(me_p > 0)
    def _():
        down.start()

    @pl.when(me_p < planes - 1)
    def _():
        up.start()

    @pl.when(me_p == 0)
    def _():
        halo_in[1] = jnp.zeros_like(halo_in[1])

    @pl.when(me_p == planes - 1)
    def _():
        halo_in[0] = jnp.zeros_like(halo_in[0])

    def send(src, dst, send_sem, recv_sem, snap, plane):
        copy = pltpu.make_async_remote_copy(
            src_ref=src, dst_ref=dst, send_sem=send_sem, recv_sem=recv_sem,
            device_id=(snap, plane), device_id_type=MESH,
        )
        copy.start()
        return copy

    shear_copies = [
        send(shear_all.at[me_s], shear_all.at[me_s], shear_send.at[d], shear_recv.at[d], peer, me_p)
        for d, peer in enumerate(snap_peers)
    ]

    images = velocity[...].reshape(slots * comps * zw, xw)
    columns[...] = jnp.dot(images, shifts, preferred_element_type=jnp.float32)
    lane = lax.broadcasted_iota(jnp.int32, (8, xw), 1)
    group = lax.div(lane, xf)
    get_stencil.wait()
    weights = {}
    for i in range(comps):
        for f in range(2):
            for a in range(3):
                k = [stencil_ref[i, a, f, b] * (1.0 / (POOL * POOL)) for b in range(3)]
                weights[i, f, a] = jnp.where(group == 0, k[1], jnp.where(group == 1, k[0], k[2]))[:1]
    for slot in range(slots):
        for i in range(comps):
            base = (slot * comps + i) * zw
            part = [columns[pl.ds(base + r, zf, stride=POOL), :] for r in range(POOL)]
            middle = part[1] + part[2]
            sums = [
                shift_rows(part[3], 1) + part[0] + middle,
                part[0] + middle + part[3],
                middle + part[3] + shift_rows(part[0], -1),
            ]
            for f in range(2):
                mixed = sum(weights[i, f, a] * sums[a] for a in range(3))
                mixed = mixed + pltpu.roll(mixed, xw - xf, 1) + pltpu.roll(mixed, xw - 2 * xf, 1)
                feats[slot, pl.ds((2 * i + f) * zf, zf), :] = mixed.astype(jnp.bfloat16)

    stream[...] = jnp.zeros_like(stream)
    get_stream.wait()
    stream[pl.ds(xw - xf, xf), :] = stream_ref[...]
    get_table.wait()
    get_block.wait()
    get_span.wait()

    def fold(value):
        return jnp.sum(value.reshape(zf // 8, 8, width), axis=0)

    first_stream = stream[pl.ds(xw - xf, xw), :]
    terms = []
    for slot in range(slots):
        proj = jnp.dot(feats[slot], first_stream, preferred_element_type=jnp.float32)
        block = block_ref[0, slot]
        term = jnp.zeros((8, width), jnp.float32)
        for i in range(comps):
            for f in range(2):
                at = (2 * i + f) * zf
                term = term + fold(proj[at : at + zf] * table[block, 3 * i + f].astype(jnp.float32))
        terms.append(term)

    for copy in shear_copies:
        copy.wait()
    every = shear_all[...]
    inner_rows = inner_all.shape[1]
    at_row = lax.broadcasted_iota(jnp.int32, (inner_rows, xw), 0)
    at_lane = lax.broadcasted_iota(jnp.int32, (inner_rows, xw), 1)
    inner = jnp.zeros((inner_rows, xw), jnp.float32)
    for a in range(snaps):
        for b in range(a, snaps):
            value = jnp.sum(every[a] * every[b])
            place = ((at_row == a) & (at_lane == b)) | ((at_row == b) & (at_lane == a))
            inner = jnp.where(place, value, inner)
    inner_all[me_p] = inner
    inner_copies = [
        send(inner_all.at[me_p], inner_all.at[me_p], inner_send.at[d], inner_recv.at[d], me_s, peer)
        for d, peer in enumerate(plane_peers)
    ]

    @pl.when(me_p > 0)
    def _():
        up.wait_recv()

    @pl.when(me_p < planes - 1)
    def _():
        down.wait_recv()

    normals = []
    for slot in range(slots):
        below = halo_in[1] if slot == 0 else pooled[slot - 1]
        above = halo_in[0]
        if slot + 1 < slots:
            above = jnp.where(slot + 1 < live_count, pooled[slot + 1], above)
        scale = span_ref[0, slot] * (1.0 / (POOL * POOL))
        normals.append(((above - below) * scale).astype(jnp.bfloat16))
    normals = jnp.concatenate(normals, axis=0)
    for i in range(comps):
        proj = jnp.dot(
            normals, stream[pl.ds(xw - xf - i * xf, xw), :], preferred_element_type=jnp.float32
        )
        for slot in range(slots):
            at = slot * zf
            tile = table[block_ref[0, slot], 3 * i + 2].astype(jnp.float32)
            terms[slot] = terms[slot] + fold(proj[at : at + zf] * tile)
    total = jnp.zeros((8, width), jnp.float32)
    for slot in range(slots):
        total = total + jnp.where(slot < live_count, terms[slot], 0.0)
    coef_all[me_p] = jnp.sum(total, axis=0, keepdims=True)
    coef_copies = [
        send(coef_all.at[me_p], coef_all.at[me_p], coef_send.at[d], coef_recv.at[d], me_s, peer)
        for d, peer in enumerate(plane_peers)
    ]

    stacked = jnp.concatenate([shear_all[s] for s in range(snaps)], axis=0)
    spare = xw - stacked.shape[0]
    if spare:
        stacked = jnp.concatenate([stacked, jnp.zeros((spare, xw), jnp.float32)], axis=0)
    shear_t[...] = stacked.T
    xl = xf // snaps
    mine = shear_t[pl.ds(me_s * xl, xl), :]
    for copy in inner_copies:
        copy.wait()
    inner = inner_all[0]
    for p in range(1, planes):
        inner = inner + inner_all[p]

    for copy in coef_copies:
        copy.wait()
    coef = coef_all[0]
    for p in range(1, planes):
        coef = coef + coef_all[p]
    coef_snap[me_s] = coef
    snap_copies = [
        send(coef_snap.at[me_s], coef_snap.at[me_s], snap_send.at[d], snap_recv.at[d], peer, me_p)
        for d, peer in enumerate(snap_peers)
    ]
    for copy in snap_copies:
        copy.wait()

    coefs = [coef_snap[s] for s in range(snaps)]
    rows = kinds * zl
    for m in range(kinds):
        for z in range(zl):
            value = jnp.zeros((xl, width), jnp.float32)
            for s in range(snaps):
                at = s * rows + m * zl + z
                value = value + mine[:, at : at + 1] * coefs[s]
            sketch_ref[m, z] = value
    weighted = jnp.zeros((inner_rows, width), jnp.float32)
    for s in range(snaps):
        weighted = weighted + inner[:, s : s + 1] * coefs[s]
    padded = coefs
    if inner_rows > snaps:
        padded = coefs + [jnp.zeros((inner_rows - snaps, width), jnp.float32)]
    stack = jnp.concatenate(padded, axis=0)
    total_rows = kinds * xf * zl * planes
    gram_ref[...] = jnp.dot(
        stack.T, weighted * (1.0 / total_rows), precision=HIGHEST,
        preferred_element_type=jnp.float32,
    )

    @pl.when(me_p > 0)
    def _():
        down.wait_send()

    @pl.when(me_p < planes - 1)
    def _():
        up.wait_send()


def per_device(
    velocity, plane_count, inv_span, kernels, omega_block, omega_table, omega_stream, wall_shear
):
    snaps, planes = lax.axis_size("snap"), lax.axis_size("plane")
    _, slots, comps, zw, xw = velocity.shape
    zf, xf = zw // POOL, xw // POOL
    width = omega_stream.shape[1]
    _, kinds, zs, _ = wall_shear.shape
    zl = zs // POOL
    inner_rows = -(-snaps // 8) * 8
    vmem = pl.BlockSpec(memory_space=pltpu.VMEM)
    hbm = pl.BlockSpec(memory_space=pltpu.HBM)
    dma = pltpu.SemaphoreType.DMA
    f32, bf16 = jnp.float32, jnp.bfloat16
    stencils = kernels.transpose(0, 2, 1, 3)
    counts = plane_count.reshape(1, -1)
    return pl.pallas_call(
        functools.partial(kernel, snaps, planes),
        out_shape=(
            jax.ShapeDtypeStruct((kinds, zl, xf // snaps, width), f32),
            jax.ShapeDtypeStruct((width, width), f32),
        ),
        in_specs=[hbm] * 8,
        out_specs=(vmem, vmem),
        scratch_shapes=[
            pltpu.SMEM(counts.shape, jnp.int32),
            pltpu.SMEM(inv_span.shape, f32),
            pltpu.SMEM(stencils.shape, f32),
            pltpu.SMEM(omega_block.shape, jnp.int32),
            pltpu.VMEM(wall_shear.shape, bf16),
            pltpu.VMEM(omega_stream.shape, bf16),
            pltpu.VMEM((slots, comps, zw, xw), bf16),
            pltpu.VMEM(omega_table.shape, bf16),
            pltpu.VMEM((2 * xw - xf, width), bf16),
            pltpu.VMEM((slots, zf, xw), f32),
            pltpu.VMEM((slots * comps * zw, xw), f32),
            pltpu.VMEM((slots, 2 * comps * zf, xw), bf16),
            pltpu.VMEM((kinds * zs, xw), f32),
            pltpu.VMEM((snaps, kinds * zl, xw), f32),
            pltpu.VMEM((xw, xw), f32),
            pltpu.VMEM((planes, inner_rows, xw), f32),
            pltpu.VMEM((2, zf, xw), f32),
            pltpu.VMEM((2, zf, xw), f32),
            pltpu.VMEM((planes, 1, width), f32),
            pltpu.VMEM((snaps, 1, width), f32),
            dma((8,)),
            dma((snaps - 1,)), dma((snaps - 1,)),
            dma((planes - 1,)), dma((planes - 1,)),
            dma((2,)), dma((2,)),
            dma((planes - 1,)), dma((planes - 1,)),
            dma((snaps - 1,)), dma((snaps - 1,)),
        ],
        compiler_params=pltpu.CompilerParams(
            collective_id=0, has_side_effects=True, vmem_limit_bytes=64 * 1024 * 1024
        ),
    )(
        counts, inv_span, stencils, omega_block, wall_shear, omega_stream, velocity, omega_table
    )


def solution(mesh):
    return jax.shard_map(
        per_device,
        mesh=mesh,
        in_specs=(
            P("snap", "plane", None, None, None),
            P("plane"),
            P("plane", None),
            P(),
            P("plane", None),
            P(),
            P(),
            P("snap", None, "plane", None),
        ),
        out_specs=(P(None, "plane", "snap", None), P()),
        check_vma=False,
    )
```

```python
import functools

import jax
import jax.numpy as jnp
from jax import lax
from jax.experimental import pallas as pl
from jax.experimental.pallas import tpu as pltpu
from jax.sharding import PartitionSpec as P

POOL = 4
MESH = pl.DeviceIdType.MESH
HIGHEST = lax.Precision.HIGHEST


def shift_rows(value, steps):
    rows = value.shape[0]
    at = lax.broadcasted_iota(jnp.int32, value.shape, 0)
    edge = 0 if steps == 1 else rows - 1
    return jnp.where(at == edge, 0.0, pltpu.roll(value, steps % rows, 0))


def kernel(
    snaps, planes,
    count_ref, span_hbm, stencil_hbm, block_hbm, shear_hbm, stream_hbm, velocity_hbm, table_hbm,
    coef_ref, mine_ref, inner_ref,
    span_ref, stencil_ref, block_ref, shear_ref, stream_ref, velocity, table, stream, pooled, columns, feats, shear_rows, shear_all, shear_t, inner_all,
    halo_out, halo_in, coef_all, coef_snap,
    local_sem, shear_send, shear_recv, inner_send, inner_recv, halo_send, halo_recv,
    coef_send, coef_recv, snap_send, snap_recv,
):
    slots, comps, zw, xw = velocity.shape
    zf, xf = zw // POOL, xw // POOL
    width = stream_hbm.shape[1]
    me_s, me_p = lax.axis_index("snap"), lax.axis_index("plane")

    snap_peers = [lax.rem(me_s + d, snaps) for d in range(1, snaps)]
    plane_peers = [lax.rem(me_p + d, planes) for d in range(1, planes)]
    barrier = pltpu.get_barrier_semaphore()
    for peer in snap_peers:
        pl.semaphore_signal(barrier, inc=1, device_id=(peer, me_p), device_id_type=MESH)
    for peer in plane_peers:
        pl.semaphore_signal(barrier, inc=1, device_id=(me_s, peer), device_id_type=MESH)

    def fetch(index, source, target):
        copy = pltpu.make_async_copy(source, target, local_sem.at[index])
        copy.start()
        return copy

    get_velocity = fetch(0, velocity_hbm.at[0], velocity)
    get_shear = fetch(1, shear_hbm, shear_ref)
    get_stencil = fetch(2, stencil_hbm, stencil_ref)
    get_span = fetch(3, span_hbm, span_ref)
    get_block = fetch(4, block_hbm, block_ref)
    get_stream = fetch(5, stream_hbm, stream_ref)
    get_table = fetch(6, table_hbm, table)

    row = lax.broadcasted_iota(jnp.int32, (comps * xw, xw), 0)
    lane = lax.broadcasted_iota(jnp.int32, (comps * xw, xw), 1)
    gap = lax.rem(row, xw) - POOL * lax.rem(lane, xf)
    hit = (lax.div(row, xw) == lax.div(lane, xf)) & (gap >= 0) & (gap < POOL)
    pack = jnp.where(hit, 1.0, 0.0).astype(jnp.bfloat16)
    row = lax.broadcasted_iota(jnp.int32, (xw, xw), 0)
    lane = lax.broadcasted_iota(jnp.int32, (xw, xw), 1)
    group = lax.div(lane, xf)
    gap = row - POOL * lax.rem(lane, xf) - jnp.where(group == 1, -1, jnp.where(group == 2, 1, 0))
    hit = (group < 3) & (gap >= 0) & (gap < POOL)
    shifts = jnp.where(hit, 1.0, 0.0).astype(jnp.bfloat16)

    kinds, zs = shear_ref.shape[1], shear_ref.shape[2]
    zl = zs // POOL
    get_shear.wait()
    shear_in = shear_ref[0].reshape(kinds * zs, xw)
    shear_rows[...] = jnp.dot(shear_in, pack[:xw], preferred_element_type=jnp.float32)
    part = [shear_rows[pl.ds(r, kinds * zl, stride=POOL), :] for r in range(POOL)]
    shear_all[me_s] = (part[0] + part[1] + part[2] + part[3]) * (1.0 / (POOL * POOL))

    get_velocity.wait()
    fields = jnp.concatenate(
        [velocity[:, i].reshape(slots * zw, xw) for i in range(comps)], axis=1
    )
    columns[pl.ds(0, slots * zw), :] = jnp.dot(fields, pack, preferred_element_type=jnp.float32)
    part = [columns[pl.ds(r, slots * zf, stride=POOL), :] for r in range(POOL)]
    pooled[...] = (part[0] + part[1] + part[2] + part[3]).reshape(slots, zf, xw)
    live_count = count_ref[0]
    halo_out[0] = pooled[0]
    last = pooled[0]
    for slot in range(1, slots):
        last = jnp.where(live_count - 1 == slot, pooled[slot], last)
    halo_out[1] = last

    pl.semaphore_wait(barrier, snaps - 1 + planes - 1)

    def halo(which, plane):
        return pltpu.make_async_remote_copy(
            src_ref=halo_out.at[which], dst_ref=halo_in.at[which],
            send_sem=halo_send.at[which], recv_sem=halo_recv.at[which],
            device_id=(me_s, plane), device_id_type=MESH,
        )

    down = halo(0, jnp.maximum(me_p - 1, 0))
    up = halo(1, jnp.minimum(me_p + 1, planes - 1))

    @pl.when(me_p > 0)
    def _():
        down.start()

    @pl.when(me_p < planes - 1)
    def _():
        up.start()

    @pl.when(me_p == 0)
    def _():
        halo_in[1] = jnp.zeros_like(halo_in[1])

    @pl.when(me_p == planes - 1)
    def _():
        halo_in[0] = jnp.zeros_like(halo_in[0])

    def send(src, dst, send_sem, recv_sem, snap, plane):
        copy = pltpu.make_async_remote_copy(
            src_ref=src, dst_ref=dst, send_sem=send_sem, recv_sem=recv_sem,
            device_id=(snap, plane), device_id_type=MESH,
        )
        copy.start()
        return copy

    shear_copies = [
        send(shear_all.at[me_s], shear_all.at[me_s], shear_send.at[d], shear_recv.at[d], peer, me_p)
        for d, peer in enumerate(snap_peers)
    ]

    images = velocity[...].reshape(slots * comps * zw, xw)
    columns[...] = jnp.dot(images, shifts, preferred_element_type=jnp.float32)
    lane = lax.broadcasted_iota(jnp.int32, (8, xw), 1)
    group = lax.div(lane, xf)
    get_stencil.wait()
    weights = {}
    for i in range(comps):
        for f in range(2):
            for a in range(3):
                k = [stencil_ref[i, a, f, b] * (1.0 / (POOL * POOL)) for b in range(3)]
                weights[i, f, a] = jnp.where(group == 0, k[1], jnp.where(group == 1, k[0], k[2]))[:1]
    for slot in range(slots):
        for i in range(comps):
            base = (slot * comps + i) * zw
            part = [columns[pl.ds(base + r, zf, stride=POOL), :] for r in range(POOL)]
            middle = part[1] + part[2]
            sums = [
                shift_rows(part[3], 1) + part[0] + middle,
                part[0] + middle + part[3],
                middle + part[3] + shift_rows(part[0], -1),
            ]
            for f in range(2):
                mixed = sum(weights[i, f, a] * sums[a] for a in range(3))
                mixed = mixed + pltpu.roll(mixed, xw - xf, 1) + pltpu.roll(mixed, xw - 2 * xf, 1)
                feats[slot, pl.ds((2 * i + f) * zf, zf), :] = mixed.astype(jnp.bfloat16)

    stream[...] = jnp.zeros_like(stream)
    get_stream.wait()
    stream[pl.ds(xw - xf, xf), :] = stream_ref[...]
    get_table.wait()
    get_block.wait()
    get_span.wait()

    def fold(value):
        return jnp.sum(value.reshape(zf // 8, 8, width), axis=0)

    first_stream = stream[pl.ds(xw - xf, xw), :]
    terms = []
    for slot in range(slots):
        proj = jnp.dot(feats[slot], first_stream, preferred_element_type=jnp.float32)
        block = block_ref[0, slot]
        term = jnp.zeros((8, width), jnp.float32)
        for i in range(comps):
            for f in range(2):
                at = (2 * i + f) * zf
                term = term + fold(proj[at : at + zf] * table[block, 3 * i + f].astype(jnp.float32))
        terms.append(term)

    @pl.when(me_p > 0)
    def _():
        up.wait_recv()

    @pl.when(me_p < planes - 1)
    def _():
        down.wait_recv()

    normals = []
    for slot in range(slots):
        below = halo_in[1] if slot == 0 else pooled[slot - 1]
        above = halo_in[0]
        if slot + 1 < slots:
            above = jnp.where(slot + 1 < live_count, pooled[slot + 1], above)
        scale = span_ref[0, slot] * (1.0 / (POOL * POOL))
        normals.append(((above - below) * scale).astype(jnp.bfloat16))
    normals = jnp.concatenate(normals, axis=0)
    for i in range(comps):
        proj = jnp.dot(
            normals, stream[pl.ds(xw - xf - i * xf, xw), :], preferred_element_type=jnp.float32
        )
        for slot in range(slots):
            at = slot * zf
            tile = table[block_ref[0, slot], 3 * i + 2].astype(jnp.float32)
            terms[slot] = terms[slot] + fold(proj[at : at + zf] * tile)
    total = jnp.zeros((8, width), jnp.float32)
    for slot in range(slots):
        total = total + jnp.where(slot < live_count, terms[slot], 0.0)
    coef_all[me_p] = jnp.sum(total, axis=0, keepdims=True)
    coef_copies = [
        send(coef_all.at[me_p], coef_all.at[me_p], coef_send.at[d], coef_recv.at[d], me_s, peer)
        for d, peer in enumerate(plane_peers)
    ]

    for copy in shear_copies:
        copy.wait()
    every = shear_all[...]
    inner_rows = inner_all.shape[1]
    at_row = lax.broadcasted_iota(jnp.int32, (inner_rows, xw), 0)
    at_lane = lax.broadcasted_iota(jnp.int32, (inner_rows, xw), 1)
    inner = jnp.zeros((inner_rows, xw), jnp.float32)
    for a in range(snaps):
        for b in range(a, snaps):
            value = jnp.sum(every[a] * every[b])
            place = ((at_row == a) & (at_lane == b)) | ((at_row == b) & (at_lane == a))
            inner = jnp.where(place, value, inner)
    inner_all[me_p] = inner
    inner_copies = [
        send(inner_all.at[me_p], inner_all.at[me_p], inner_send.at[d], inner_recv.at[d], me_s, peer)
        for d, peer in enumerate(plane_peers)
    ]

    stacked = jnp.concatenate([shear_all[s] for s in range(snaps)], axis=0)
    spare = xw - stacked.shape[0]
    if spare:
        stacked = jnp.concatenate([stacked, jnp.zeros((spare, xw), jnp.float32)], axis=0)
    shear_t[...] = stacked.T
    xl = xf // snaps
    mine_ref[...] = shear_t[pl.ds(me_s * xl, xl), :]
    for copy in coef_copies:
        copy.wait()
    coef = coef_all[0]
    for p in range(1, planes):
        coef = coef + coef_all[p]
    coef_snap[me_s] = coef
    snap_copies = [
        send(coef_snap.at[me_s], coef_snap.at[me_s], snap_send.at[d], snap_recv.at[d], peer, me_p)
        for d, peer in enumerate(snap_peers)
    ]
    for copy in inner_copies:
        copy.wait()
    inner = inner_all[0]
    for p in range(1, planes):
        inner = inner + inner_all[p]

    inner_ref[...] = inner
    for copy in snap_copies:
        copy.wait()
    coef_ref[...] = jnp.concatenate([coef_snap[s] for s in range(snaps)], axis=0)

    @pl.when(me_p > 0)
    def _():
        down.wait_send()

    @pl.when(me_p < planes - 1)
    def _():
        up.wait_send()


def outputs_kernel(
    planes, coef_ref, mine_ref, inner_ref, sketch_hbm, gram_hbm, sketch_ref, gram_ref, sems
):
    snaps, width = coef_ref.shape
    kinds, zl, xl, _ = sketch_ref.shape
    inner_rows = inner_ref.shape[0]
    mine, inner = mine_ref[...], inner_ref[...]
    coefs = [coef_ref[pl.ds(s, 1), :] for s in range(snaps)]
    rows = kinds * zl
    for m in range(kinds):
        for z in range(zl):
            value = jnp.zeros((xl, width), jnp.float32)
            for s in range(snaps):
                at = s * rows + m * zl + z
                value = value + mine[:, at : at + 1] * coefs[s]
            sketch_ref[m, z] = value
    put_sketch = pltpu.make_async_copy(sketch_ref, sketch_hbm, sems.at[0])
    put_sketch.start()
    weighted = jnp.zeros((inner_rows, width), jnp.float32)
    for s in range(snaps):
        weighted = weighted + inner[:, s : s + 1] * coefs[s]
    padded = coefs
    if inner_rows > snaps:
        padded = coefs + [jnp.zeros((inner_rows - snaps, width), jnp.float32)]
    stack = jnp.concatenate(padded, axis=0)
    total_rows = kinds * (xl * snaps) * zl * planes
    gram_ref[...] = jnp.dot(
        stack.T, weighted * (1.0 / total_rows), precision=HIGHEST,
        preferred_element_type=jnp.float32,
    )
    put_gram = pltpu.make_async_copy(gram_ref, gram_hbm, sems.at[1])
    put_gram.start()
    put_sketch.wait()
    put_gram.wait()


def per_device(
    velocity, plane_count, inv_span, kernels, omega_block, omega_table, omega_stream, wall_shear
):
    snaps, planes = lax.axis_size("snap"), lax.axis_size("plane")
    _, slots, comps, zw, xw = velocity.shape
    zf, xf = zw // POOL, xw // POOL
    width = omega_stream.shape[1]
    _, kinds, zs, _ = wall_shear.shape
    zl = zs // POOL
    inner_rows = -(-snaps // 8) * 8
    vmem = pl.BlockSpec(memory_space=pltpu.VMEM)
    hbm = pl.BlockSpec(memory_space=pltpu.HBM)
    dma = pltpu.SemaphoreType.DMA
    f32, bf16 = jnp.float32, jnp.bfloat16
    stencils = kernels.transpose(0, 2, 1, 3)
    coef, mine, inner = pl.pallas_call(
        functools.partial(kernel, snaps, planes),
        out_shape=(
            jax.ShapeDtypeStruct((snaps, width), f32),
            jax.ShapeDtypeStruct((xf // snaps, xw), f32),
            jax.ShapeDtypeStruct((inner_rows, xw), f32),
        ),
        in_specs=[pl.BlockSpec(memory_space=pltpu.SMEM)] + [hbm] * 7,
        out_specs=(vmem, vmem, vmem),
        scratch_shapes=[
            pltpu.SMEM(inv_span.shape, f32),
            pltpu.SMEM(stencils.shape, f32),
            pltpu.SMEM(omega_block.shape, jnp.int32),
            pltpu.VMEM(wall_shear.shape, bf16),
            pltpu.VMEM(omega_stream.shape, bf16),
            pltpu.VMEM((slots, comps, zw, xw), bf16),
            pltpu.VMEM(omega_table.shape, bf16),
            pltpu.VMEM((2 * xw - xf, width), bf16),
            pltpu.VMEM((slots, zf, xw), f32),
            pltpu.VMEM((slots * comps * zw, xw), f32),
            pltpu.VMEM((slots, 2 * comps * zf, xw), bf16),
            pltpu.VMEM((kinds * zs, xw), f32),
            pltpu.VMEM((snaps, kinds * zl, xw), f32),
            pltpu.VMEM((xw, xw), f32),
            pltpu.VMEM((planes, inner_rows, xw), f32),
            pltpu.VMEM((2, zf, xw), f32),
            pltpu.VMEM((2, zf, xw), f32),
            pltpu.VMEM((planes, 1, width), f32),
            pltpu.VMEM((snaps, 1, width), f32),
            dma((7,)),
            dma((snaps - 1,)), dma((snaps - 1,)),
            dma((planes - 1,)), dma((planes - 1,)),
            dma((2,)), dma((2,)),
            dma((planes - 1,)), dma((planes - 1,)),
            dma((snaps - 1,)), dma((snaps - 1,)),
        ],
        compiler_params=pltpu.CompilerParams(
            collective_id=0, has_side_effects=True, vmem_limit_bytes=24 * 1024 * 1024
        ),
    )(
        plane_count,
        *(
            pltpu.with_memory_space_constraint(value, pltpu.HBM)
            for value in (
                inv_span, stencils, omega_block, wall_shear, omega_stream, velocity, omega_table
            )
        )
    )
    sketch_shape = (kinds, zl, xf // snaps, width)
    return pl.pallas_call(
        functools.partial(outputs_kernel, planes),
        out_shape=(pltpu.HBM(sketch_shape, f32), pltpu.HBM((width, width), f32)),
        in_specs=[vmem] * 3,
        out_specs=(hbm, hbm),
        scratch_shapes=[
            pltpu.VMEM(sketch_shape, f32), pltpu.VMEM((width, width), f32), dma((2,)),
        ],
    )(coef, mine, inner)


def solution(mesh):
    return jax.shard_map(
        per_device,
        mesh=mesh,
        in_specs=(
            P("snap", "plane", None, None, None),
            P("plane"),
            P("plane", None),
            P(),
            P("plane", None),
            P(),
            P(),
            P("snap", None, "plane", None),
        ),
        out_specs=(P(None, "plane", "snap", None), P()),
        check_vma=False,
    )
```

```python
import functools

import jax
import jax.numpy as jnp
from jax import lax
from jax.experimental import pallas as pl
from jax.experimental.pallas import tpu as pltpu
from jax.sharding import PartitionSpec as P

POOL = 4
MESH = pl.DeviceIdType.MESH
HIGHEST = lax.Precision.HIGHEST


def shift_rows(value, steps):
    rows = value.shape[0]
    at = lax.broadcasted_iota(jnp.int32, value.shape, 0)
    edge = 0 if steps == 1 else rows - 1
    return jnp.where(at == edge, 0.0, pltpu.roll(value, steps % rows, 0))


def kernel(
    snaps, planes, everyone,
    count_ref, span_hbm, stencil_hbm, block_hbm, shear_hbm, stream_hbm, velocity_hbm, table_hbm,
    coef_ref, mine_ref, inner_ref,
    span_ref, stencil_ref, block_ref, shear_ref, stream_ref, velocity, table, stream, pooled, columns, feats, shear_rows, shear_all, shear_t, inner_all,
    halo_out, halo_in, coef_all, coef_snap,
    local_sem, shear_send, shear_recv, inner_send, inner_recv, halo_send, halo_recv,
    coef_send, coef_recv, snap_send, snap_recv,
):
    slots, comps, zw, xw = velocity.shape
    zf, xf = zw // POOL, xw // POOL
    width = stream_hbm.shape[1]
    me_s, me_p = lax.axis_index("snap"), lax.axis_index("plane")

    def fetch(index, source, target):
        copy = pltpu.make_async_copy(source, target, local_sem.at[index])
        copy.start()
        return copy

    get_velocity = fetch(0, velocity_hbm.at[0], velocity)
    get_shear = fetch(1, shear_hbm, shear_ref)
    snap_peers = [lax.rem(me_s + d, snaps) for d in range(1, snaps)]
    plane_peers = [lax.rem(me_p + d, planes) for d in range(1, planes)]
    if everyone:
        greeted = [
            (me_s if ds == 0 else snap_peers[ds - 1], me_p if dp == 0 else plane_peers[dp - 1])
            for dp in range(planes)
            for ds in range(snaps)
            if ds + dp > 0
        ]
    else:
        greeted = [(peer, me_p) for peer in snap_peers] + [(me_s, peer) for peer in plane_peers]
    barrier = pltpu.get_barrier_semaphore()
    for peer in greeted:
        pl.semaphore_signal(barrier, inc=1, device_id=peer, device_id_type=MESH)

    get_stencil = fetch(2, stencil_hbm, stencil_ref)
    get_span = fetch(3, span_hbm, span_ref)
    get_block = fetch(4, block_hbm, block_ref)
    get_stream = fetch(5, stream_hbm, stream_ref)
    get_table = fetch(6, table_hbm, table)

    row = lax.broadcasted_iota(jnp.int32, (xw, xw), 0)
    lane = lax.broadcasted_iota(jnp.int32, (xw, xw), 1)

    def windows(start):
        gap = row - start
        return jnp.where((gap >= 0) & (gap < POOL), 1.0, 0.0).astype(jnp.bfloat16)

    pack = jnp.concatenate([windows(POOL * (lane - xf * i)) for i in range(comps)], axis=0)
    first = jnp.where(lane < xf, 0, jnp.where(lane < 2 * xf, -1 - POOL * xf, 1 - 2 * POOL * xf))
    shifts = windows(POOL * lane + first)

    kinds, zs = shear_ref.shape[1], shear_ref.shape[2]
    zl = zs // POOL
    get_shear.wait()
    shear_in = shear_ref[0].reshape(kinds * zs, xw)
    shear_rows[...] = jnp.dot(shear_in, pack[:xw], preferred_element_type=jnp.float32)
    part = [shear_rows[pl.ds(r, kinds * zl, stride=POOL), :] for r in range(POOL)]
    shear_all[me_s] = (part[0] + part[1] + part[2] + part[3]) * (1.0 / (POOL * POOL))

    get_velocity.wait()
    fields = jnp.concatenate(
        [velocity[:, i].reshape(slots * zw, xw) for i in range(comps)], axis=1
    )
    columns[pl.ds(0, slots * zw), :] = jnp.dot(fields, pack, preferred_element_type=jnp.float32)
    part = [columns[pl.ds(r, slots * zf, stride=POOL), :] for r in range(POOL)]
    pooled[...] = (part[0] + part[1] + part[2] + part[3]).reshape(slots, zf, xw)
    live_count = count_ref[0]
    halo_out[0] = pooled[0]
    last = pooled[0]
    for slot in range(1, slots):
        last = jnp.where(live_count - 1 == slot, pooled[slot], last)
    halo_out[1] = last

    pl.semaphore_wait(barrier, len(greeted))

    def halo(which, plane):
        return pltpu.make_async_remote_copy(
            src_ref=halo_out.at[which], dst_ref=halo_in.at[which],
            send_sem=halo_send.at[which], recv_sem=halo_recv.at[which],
            device_id=(me_s, plane), device_id_type=MESH,
        )

    down = halo(0, jnp.maximum(me_p - 1, 0))
    up = halo(1, jnp.minimum(me_p + 1, planes - 1))

    @pl.when(me_p > 0)
    def _():
        down.start()

    @pl.when(me_p < planes - 1)
    def _():
        up.start()

    @pl.when(me_p == 0)
    def _():
        halo_in[1] = jnp.zeros_like(halo_in[1])

    @pl.when(me_p == planes - 1)
    def _():
        halo_in[0] = jnp.zeros_like(halo_in[0])

    def send(src, dst, send_sem, recv_sem, snap, plane):
        copy = pltpu.make_async_remote_copy(
            src_ref=src, dst_ref=dst, send_sem=send_sem, recv_sem=recv_sem,
            device_id=(snap, plane), device_id_type=MESH,
        )
        copy.start()
        return copy

    shear_copies = [
        send(shear_all.at[me_s], shear_all.at[me_s], shear_send.at[d], shear_recv.at[d], peer, me_p)
        for d, peer in enumerate(snap_peers)
    ]

    images = velocity[...].reshape(slots * comps * zw, xw)
    columns[...] = jnp.dot(images, shifts, preferred_element_type=jnp.float32)
    lane = lax.broadcasted_iota(jnp.int32, (8, xw), 1)
    get_stencil.wait()
    weights = {}
    for i in range(comps):
        for f in range(2):
            for a in range(3):
                k = [stencil_ref[i, a, f, b] * (1.0 / (POOL * POOL)) for b in range(3)]
                weights[i, f, a] = jnp.where(lane < xf, k[1], jnp.where(lane < 2 * xf, k[0], k[2]))[:1]
    for slot in range(slots):
        for i in range(comps):
            base = (slot * comps + i) * zw
            part = [columns[pl.ds(base + r, zf, stride=POOL), :] for r in range(POOL)]
            middle = part[1] + part[2]
            sums = [
                shift_rows(part[3], 1) + part[0] + middle,
                part[0] + middle + part[3],
                middle + part[3] + shift_rows(part[0], -1),
            ]
            for f in range(2):
                mixed = sum(weights[i, f, a] * sums[a] for a in range(3))
                mixed = mixed + pltpu.roll(mixed, xw - xf, 1) + pltpu.roll(mixed, xw - 2 * xf, 1)
                feats[slot, pl.ds((2 * i + f) * zf, zf), :] = mixed.astype(jnp.bfloat16)

    stream[...] = jnp.zeros_like(stream)
    get_stream.wait()
    stream[pl.ds(xw - xf, xf), :] = stream_ref[...]
    get_table.wait()
    get_block.wait()
    get_span.wait()

    def fold(value):
        return jnp.sum(value.reshape(zf // 8, 8, width), axis=0)

    first_stream = stream[pl.ds(xw - xf, xw), :]
    terms = []
    for slot in range(slots):
        proj = jnp.dot(feats[slot], first_stream, preferred_element_type=jnp.float32)
        block = block_ref[0, slot]
        term = jnp.zeros((8, width), jnp.float32)
        for i in range(comps):
            for f in range(2):
                at = (2 * i + f) * zf
                term = term + fold(proj[at : at + zf] * table[block, 3 * i + f].astype(jnp.float32))
        terms.append(term)

    @pl.when(me_p > 0)
    def _():
        up.wait_recv()

    @pl.when(me_p < planes - 1)
    def _():
        down.wait_recv()

    normals = []
    for slot in range(slots):
        below = halo_in[1] if slot == 0 else pooled[slot - 1]
        above = halo_in[0]
        if slot + 1 < slots:
            above = jnp.where(slot + 1 < live_count, pooled[slot + 1], above)
        scale = span_ref[0, slot] * (1.0 / (POOL * POOL))
        normals.append(((above - below) * scale).astype(jnp.bfloat16))
    normals = jnp.concatenate(normals, axis=0)
    for i in range(comps):
        proj = jnp.dot(
            normals, stream[pl.ds(xw - xf - i * xf, xw), :], preferred_element_type=jnp.float32
        )
        for slot in range(slots):
            at = slot * zf
            tile = table[block_ref[0, slot], 3 * i + 2].astype(jnp.float32)
            terms[slot] = terms[slot] + fold(proj[at : at + zf] * tile)
    total = jnp.zeros((8, width), jnp.float32)
    for slot in range(slots):
        total = total + jnp.where(slot < live_count, terms[slot], 0.0)
    coef_all[me_s, me_p] = jnp.sum(total, axis=0, keepdims=True)
    receivers = greeted if everyone else [(me_s, peer) for peer in plane_peers]
    mine = coef_all.at[me_s, me_p]
    coef_copies = [
        send(mine, mine, coef_send.at[d], coef_recv.at[d], *peer)
        for d, peer in enumerate(receivers)
    ]

    for copy in shear_copies:
        copy.wait()
    every = shear_all[...]
    at_lane = lax.broadcasted_iota(jnp.int32, (snaps, xw), 1)
    inner = jnp.zeros((snaps, xw), jnp.float32)
    for a in range(snaps):
        column = jnp.sum(jnp.sum(every * every[a][None], axis=1), axis=1, keepdims=True)
        inner = jnp.where(at_lane == a, column, inner)
    inner_all[me_p] = inner
    inner_copies = [
        send(inner_all.at[me_p], inner_all.at[me_p], inner_send.at[d], inner_recv.at[d], me_s, peer)
        for d, peer in enumerate(plane_peers)
    ]

    stacked = jnp.concatenate([shear_all[s] for s in range(snaps)], axis=0)
    spare = xw - stacked.shape[0]
    if spare:
        stacked = jnp.concatenate([stacked, jnp.zeros((spare, xw), jnp.float32)], axis=0)
    shear_t[...] = stacked.T
    xl = xf // snaps
    mine_ref[...] = shear_t[pl.ds(me_s * xl, xl), :]
    if not everyone:
        for copy in coef_copies:
            copy.wait()
        coef = coef_all[me_s, 0]
        for p in range(1, planes):
            coef = coef + coef_all[me_s, p]
        coef_snap[me_s] = coef
        coef_copies = [
            send(
                coef_snap.at[me_s], coef_snap.at[me_s], snap_send.at[d], snap_recv.at[d], peer, me_p
            )
            for d, peer in enumerate(snap_peers)
        ]
    for copy in inner_copies:
        copy.wait()
    inner = inner_all[0]
    for p in range(1, planes):
        inner = inner + inner_all[p]

    inner_ref[...] = inner
    for copy in coef_copies:
        copy.wait()
    if everyone:
        for s in range(snaps):
            coef = coef_all[s, 0]
            for p in range(1, planes):
                coef = coef + coef_all[s, p]
            coef_ref[pl.ds(s, 1), :] = coef
    else:
        coef_ref[...] = jnp.concatenate([coef_snap[s] for s in range(snaps)], axis=0)

    @pl.when(me_p > 0)
    def _():
        down.wait_send()

    @pl.when(me_p < planes - 1)
    def _():
        up.wait_send()


def outputs_kernel(
    planes, coef_ref, mine_ref, inner_ref, sketch_hbm, gram_hbm, sketch_ref, gram_ref, sems
):
    snaps, width = coef_ref.shape
    kinds, zl, xl, _ = sketch_ref.shape
    padding = -snaps % 8
    mine, inner = mine_ref[...], inner_ref[...]
    coefs = [coef_ref[pl.ds(s, 1), :] for s in range(snaps)]
    rows = kinds * zl
    for m in range(kinds):
        for z in range(zl):
            value = jnp.zeros((xl, width), jnp.float32)
            for s in range(snaps):
                at = s * rows + m * zl + z
                value = value + mine[:, at : at + 1] * coefs[s]
            sketch_ref[m, z] = value
    put_sketch = pltpu.make_async_copy(sketch_ref, sketch_hbm, sems.at[0])
    put_sketch.start()
    weighted = jnp.zeros((snaps, width), jnp.float32)
    for s in range(snaps):
        weighted = weighted + inner[:, s : s + 1] * coefs[s]
    stack = coef_ref[...]
    if padding:
        stack = jnp.concatenate([stack, jnp.zeros((padding, width), jnp.float32)], axis=0)
        weighted = jnp.concatenate([weighted, jnp.zeros((padding, width), jnp.float32)], axis=0)
    total_rows = kinds * (xl * snaps) * zl * planes
    gram_ref[...] = jnp.dot(
        stack.T, weighted * (1.0 / total_rows), precision=HIGHEST,
        preferred_element_type=jnp.float32,
    )
    put_gram = pltpu.make_async_copy(gram_ref, gram_hbm, sems.at[1])
    put_gram.start()
    put_sketch.wait()
    put_gram.wait()


def per_device(
    velocity, plane_count, inv_span, kernels, omega_block, omega_table, omega_stream, wall_shear
):
    snaps, planes = lax.axis_size("snap"), lax.axis_size("plane")
    _, slots, comps, zw, xw = velocity.shape
    zf, xf = zw // POOL, xw // POOL
    width = omega_stream.shape[1]
    _, kinds, zs, _ = wall_shear.shape
    zl = zs // POOL
    everyone = snaps * planes <= 64
    receivers = (snaps * planes if everyone else planes) - 1
    vmem = pl.BlockSpec(memory_space=pltpu.VMEM)
    hbm = pl.BlockSpec(memory_space=pltpu.HBM)
    dma = pltpu.SemaphoreType.DMA
    f32, bf16 = jnp.float32, jnp.bfloat16
    stencils = kernels.transpose(0, 2, 1, 3)
    coef, mine, inner = pl.pallas_call(
        functools.partial(kernel, snaps, planes, everyone),
        out_shape=(
            jax.ShapeDtypeStruct((snaps, width), f32),
            jax.ShapeDtypeStruct((xf // snaps, xw), f32),
            jax.ShapeDtypeStruct((snaps, xw), f32),
        ),
        in_specs=[pl.BlockSpec(memory_space=pltpu.SMEM)] + [hbm] * 7,
        out_specs=(vmem, vmem, vmem),
        scratch_shapes=[
            pltpu.SMEM(inv_span.shape, f32),
            pltpu.SMEM(stencils.shape, f32),
            pltpu.SMEM(omega_block.shape, jnp.int32),
            pltpu.VMEM(wall_shear.shape, bf16),
            pltpu.VMEM(omega_stream.shape, bf16),
            pltpu.VMEM((slots, comps, zw, xw), bf16),
            pltpu.VMEM(omega_table.shape, bf16),
            pltpu.VMEM((2 * xw - xf, width), bf16),
            pltpu.VMEM((slots, zf, xw), f32),
            pltpu.VMEM((slots * comps * zw, xw), f32),
            pltpu.VMEM((slots, 2 * comps * zf, xw), bf16),
            pltpu.VMEM((kinds * zs, xw), f32),
            pltpu.VMEM((snaps, kinds * zl, xw), f32),
            pltpu.VMEM((xw, xw), f32),
            pltpu.VMEM((planes, snaps, xw), f32),
            pltpu.VMEM((2, zf, xw), f32),
            pltpu.VMEM((2, zf, xw), f32),
            pltpu.VMEM((snaps, planes, 1, width), f32),
            pltpu.VMEM((snaps, 1, width), f32),
            dma((7,)),
            dma((snaps - 1,)), dma((snaps - 1,)),
            dma((planes - 1,)), dma((planes - 1,)),
            dma((2,)), dma((2,)),
            dma((receivers,)), dma((receivers,)),
            dma((snaps - 1,)), dma((snaps - 1,)),
        ],
        compiler_params=pltpu.CompilerParams(
            collective_id=0, has_side_effects=True, vmem_limit_bytes=24 * 1024 * 1024
        ),
    )(
        plane_count,
        *(
            pltpu.with_memory_space_constraint(value, pltpu.HBM)
            for value in (
                inv_span, stencils, omega_block, wall_shear, omega_stream, velocity, omega_table
            )
        )
    )
    sketch_shape = (kinds, zl, xf // snaps, width)
    return pl.pallas_call(
        functools.partial(outputs_kernel, planes),
        out_shape=(pltpu.HBM(sketch_shape, f32), pltpu.HBM((width, width), f32)),
        in_specs=[vmem] * 3,
        out_specs=(hbm, hbm),
        scratch_shapes=[
            pltpu.VMEM(sketch_shape, f32), pltpu.VMEM((width, width), f32), dma((2,)),
        ],
        compiler_params=pltpu.CompilerParams(vmem_limit_bytes=16 * 1024 * 1024),
    )(coef, mine, inner)


def solution(mesh):
    return jax.shard_map(
        per_device,
        mesh=mesh,
        in_specs=(
            P("snap", "plane", None, None, None),
            P("plane"),
            P("plane", None),
            P(),
            P("plane", None),
            P(),
            P(),
            P("snap", None, "plane", None),
        ),
        out_specs=(P(None, "plane", "snap", None), P()),
        check_vma=False,
    )
```

```python
import functools

import jax
import jax.numpy as jnp
from jax import lax
from jax.experimental import pallas as pl
from jax.experimental.pallas import tpu as pltpu
from jax.sharding import PartitionSpec as P

POOL = 4
MESH = pl.DeviceIdType.MESH
HIGHEST = lax.Precision.HIGHEST


def shift_rows(value, steps):
    rows = value.shape[0]
    at = lax.broadcasted_iota(jnp.int32, value.shape, 0)
    edge = 0 if steps == 1 else rows - 1
    return jnp.where(at == edge, 0.0, pltpu.roll(value, steps % rows, 0))


def kernel(
    snaps, planes, everyone,
    count_ref, span_hbm, stencil_hbm, block_hbm, shear_hbm, stream_hbm, velocity_hbm, table_hbm,
    coef_ref, mine_ref, inner_ref,
    span_ref, stencil_ref, block_ref, shear_ref, stream_ref, velocity, table, stream, pooled, columns, feats, shear_rows, shear_all, shear_t, inner_all,
    halo_out, halo_in, coef_all, coef_snap,
    local_sem, shear_send, shear_recv, inner_send, inner_recv, halo_send, halo_recv,
    coef_send, coef_recv, snap_send, snap_recv,
):
    slots, comps, zw, xw = velocity.shape
    zf, xf = zw // POOL, xw // POOL
    width = stream_hbm.shape[1]
    me_s, me_p = lax.axis_index("snap"), lax.axis_index("plane")

    def fetch(index, source, target):
        copy = pltpu.make_async_copy(source, target, local_sem.at[index])
        copy.start()
        return copy

    get_velocity = fetch(0, velocity_hbm.at[0], velocity)
    get_shear = fetch(1, shear_hbm, shear_ref)
    snap_peers = [lax.rem(me_s + d, snaps) for d in range(1, snaps)]
    plane_peers = [lax.rem(me_p + d, planes) for d in range(1, planes)]
    if everyone:
        greeted = [
            (me_s if ds == 0 else snap_peers[ds - 1], me_p if dp == 0 else plane_peers[dp - 1])
            for dp in range(planes)
            for ds in range(snaps)
            if ds + dp > 0
        ]
    else:
        greeted = [(peer, me_p) for peer in snap_peers] + [(me_s, peer) for peer in plane_peers]
    barrier = pltpu.get_barrier_semaphore()
    for peer in greeted:
        pl.semaphore_signal(barrier, inc=1, device_id=peer, device_id_type=MESH)

    get_stencil = fetch(2, stencil_hbm, stencil_ref)
    get_span = fetch(3, span_hbm, span_ref)
    get_block = fetch(4, block_hbm, block_ref)
    get_stream = fetch(5, stream_hbm, stream_ref)
    get_table = fetch(6, table_hbm, table)

    row = lax.broadcasted_iota(jnp.int32, (xw, xw), 0)
    lane = lax.broadcasted_iota(jnp.int32, (xw, xw), 1)

    def windows(start):
        gap = row - start
        return jnp.where((gap >= 0) & (gap < POOL), 1.0, 0.0).astype(jnp.bfloat16)

    pack = jnp.concatenate([windows(POOL * (lane - xf * i)) for i in range(comps)], axis=0)
    first = jnp.where(lane < xf, 0, jnp.where(lane < 2 * xf, -1 - POOL * xf, 1 - 2 * POOL * xf))
    shifts = windows(POOL * lane + first)

    get_velocity.wait()
    fields = jnp.concatenate(
        [velocity[:, i].reshape(slots * zw, xw) for i in range(comps)], axis=1
    )
    columns[pl.ds(0, slots * zw), :] = jnp.dot(fields, pack, preferred_element_type=jnp.float32)
    part = [columns[pl.ds(r, slots * zf, stride=POOL), :] for r in range(POOL)]
    pooled[...] = (part[0] + part[1] + part[2] + part[3]).reshape(slots, zf, xw)
    live_count = count_ref[0]
    halo_out[0] = pooled[0]
    last = pooled[0]
    for slot in range(1, slots):
        last = jnp.where(live_count - 1 == slot, pooled[slot], last)
    halo_out[1] = last

    pl.semaphore_wait(barrier, len(greeted))

    def halo(which, plane):
        return pltpu.make_async_remote_copy(
            src_ref=halo_out.at[which], dst_ref=halo_in.at[which],
            send_sem=halo_send.at[which], recv_sem=halo_recv.at[which],
            device_id=(me_s, plane), device_id_type=MESH,
        )

    down = halo(0, jnp.maximum(me_p - 1, 0))
    up = halo(1, jnp.minimum(me_p + 1, planes - 1))

    @pl.when(me_p > 0)
    def _():
        down.start()

    @pl.when(me_p < planes - 1)
    def _():
        up.start()

    @pl.when(me_p == 0)
    def _():
        halo_in[1] = jnp.zeros_like(halo_in[1])

    @pl.when(me_p == planes - 1)
    def _():
        halo_in[0] = jnp.zeros_like(halo_in[0])

    kinds, zs = shear_ref.shape[1], shear_ref.shape[2]
    zl = zs // POOL
    get_shear.wait()
    shear_in = shear_ref[0].reshape(kinds * zs, xw)
    shear_rows[...] = jnp.dot(shear_in, pack[:xw], preferred_element_type=jnp.float32)
    part = [shear_rows[pl.ds(r, kinds * zl, stride=POOL), :] for r in range(POOL)]
    shear_all[me_s] = (part[0] + part[1] + part[2] + part[3]) * (1.0 / (POOL * POOL))

    def send(src, dst, send_sem, recv_sem, snap, plane):
        copy = pltpu.make_async_remote_copy(
            src_ref=src, dst_ref=dst, send_sem=send_sem, recv_sem=recv_sem,
            device_id=(snap, plane), device_id_type=MESH,
        )
        copy.start()
        return copy

    shear_copies = [
        send(shear_all.at[me_s], shear_all.at[me_s], shear_send.at[d], shear_recv.at[d], peer, me_p)
        for d, peer in enumerate(snap_peers)
    ]

    images = velocity[...].reshape(slots * comps * zw, xw)
    columns[...] = jnp.dot(images, shifts, preferred_element_type=jnp.float32)
    lane = lax.broadcasted_iota(jnp.int32, (8, xw), 1)
    get_stencil.wait()
    weights = {}
    for i in range(comps):
        for f in range(2):
            for a in range(3):
                k = [stencil_ref[i, a, f, b] * (1.0 / (POOL * POOL)) for b in range(3)]
                weights[i, f, a] = jnp.where(lane < xf, k[1], jnp.where(lane < 2 * xf, k[0], k[2]))[:1]
    for slot in range(slots):
        for i in range(comps):
            base = (slot * comps + i) * zw
            part = [columns[pl.ds(base + r, zf, stride=POOL), :] for r in range(POOL)]
            middle = part[1] + part[2]
            sums = [
                shift_rows(part[3], 1) + part[0] + middle,
                part[0] + middle + part[3],
                middle + part[3] + shift_rows(part[0], -1),
            ]
            for f in range(2):
                mixed = sum(weights[i, f, a] * sums[a] for a in range(3))
                mixed = mixed + pltpu.roll(mixed, xw - xf, 1) + pltpu.roll(mixed, xw - 2 * xf, 1)
                feats[slot, pl.ds((2 * i + f) * zf, zf), :] = mixed.astype(jnp.bfloat16)

    stream[...] = jnp.zeros_like(stream)
    get_stream.wait()
    stream[pl.ds(xw - xf, xf), :] = stream_ref[...]
    get_table.wait()
    get_block.wait()
    get_span.wait()

    def fold(value):
        return jnp.sum(value.reshape(zf // 8, 8, width), axis=0)

    first_stream = stream[pl.ds(xw - xf, xw), :]
    terms = []
    for slot in range(slots):
        proj = jnp.dot(feats[slot], first_stream, preferred_element_type=jnp.float32)
        block = block_ref[0, slot]
        term = jnp.zeros((8, width), jnp.float32)
        for i in range(comps):
            for f in range(2):
                at = (2 * i + f) * zf
                term = term + fold(proj[at : at + zf] * table[block, 3 * i + f].astype(jnp.float32))
        terms.append(term)

    @pl.when(me_p > 0)
    def _():
        up.wait_recv()

    @pl.when(me_p < planes - 1)
    def _():
        down.wait_recv()

    normals = []
    for slot in range(slots):
        below = halo_in[1] if slot == 0 else pooled[slot - 1]
        above = halo_in[0]
        if slot + 1 < slots:
            above = jnp.where(slot + 1 < live_count, pooled[slot + 1], above)
        scale = span_ref[0, slot] * (1.0 / (POOL * POOL))
        normals.append(((above - below) * scale).astype(jnp.bfloat16))
    normals = jnp.concatenate(normals, axis=0)
    for i in range(comps):
        proj = jnp.dot(
            normals, stream[pl.ds(xw - xf - i * xf, xw), :], preferred_element_type=jnp.float32
        )
        for slot in range(slots):
            at = slot * zf
            tile = table[block_ref[0, slot], 3 * i + 2].astype(jnp.float32)
            terms[slot] = terms[slot] + fold(proj[at : at + zf] * tile)
    total = jnp.zeros((8, width), jnp.float32)
    for slot in range(slots):
        total = total + jnp.where(slot < live_count, terms[slot], 0.0)
    slot_of_mine = me_s * planes + me_p
    coef_all[slot_of_mine] = jnp.sum(total, axis=0, keepdims=True)
    receivers = greeted if everyone else [(me_s, peer) for peer in plane_peers]
    mine = coef_all.at[slot_of_mine]
    coef_copies = [
        send(
            mine, mine, coef_send.at[0 if everyone else d], coef_recv.at[0 if everyone else d], *peer
        )
        for d, peer in enumerate(receivers)
    ]

    for copy in shear_copies:
        copy.wait()
    every = shear_all[...]
    at_lane = lax.broadcasted_iota(jnp.int32, (snaps, xw), 1)
    inner = jnp.zeros((snaps, xw), jnp.float32)
    for a in range(snaps):
        column = jnp.sum(jnp.sum(every * every[a][None], axis=1), axis=1, keepdims=True)
        inner = jnp.where(at_lane == a, column, inner)
    inner_all[me_p] = inner
    inner_copies = [
        send(inner_all.at[me_p], inner_all.at[me_p], inner_send.at[d], inner_recv.at[d], me_s, peer)
        for d, peer in enumerate(plane_peers)
    ]

    stacked = jnp.concatenate([shear_all[s] for s in range(snaps)], axis=0)
    spare = xw - stacked.shape[0]
    if spare:
        stacked = jnp.concatenate([stacked, jnp.zeros((spare, xw), jnp.float32)], axis=0)
    shear_t[...] = stacked.T
    xl = xf // snaps
    mine_ref[...] = shear_t[pl.ds(me_s * xl, xl), :]
    if not everyone:
        for copy in coef_copies:
            copy.wait()
        coef = coef_all[me_s * planes]
        for p in range(1, planes):
            coef = coef + coef_all[me_s * planes + p]
        coef_snap[me_s] = coef
        coef_copies = [
            send(
                coef_snap.at[me_s], coef_snap.at[me_s], snap_send.at[d], snap_recv.at[d], peer, me_p
            )
            for d, peer in enumerate(snap_peers)
        ]
    for copy in inner_copies:
        copy.wait()
    inner = inner_all[0]
    for p in range(1, planes):
        inner = inner + inner_all[p]

    inner_ref[...] = inner
    if everyone:
        several = coef_all.at[pl.ds(0, len(receivers))]
        pltpu.make_async_copy(several, several, coef_send.at[0]).wait()
        pltpu.make_async_copy(several, several, coef_recv.at[0]).wait()
        for s in range(snaps):
            coef = coef_all[s * planes]
            for p in range(1, planes):
                coef = coef + coef_all[s * planes + p]
            coef_ref[pl.ds(s, 1), :] = coef
    else:
        for copy in coef_copies:
            copy.wait()
        coef_ref[...] = jnp.concatenate([coef_snap[s] for s in range(snaps)], axis=0)

    @pl.when(me_p > 0)
    def _():
        down.wait_send()

    @pl.when(me_p < planes - 1)
    def _():
        up.wait_send()


def outputs_kernel(
    planes, coef_ref, mine_ref, inner_ref, sketch_hbm, gram_hbm, sketch_ref, gram_ref, sems
):
    snaps, width = coef_ref.shape
    kinds, zl, xl, _ = sketch_ref.shape
    padding = -snaps % 8
    mine, inner = mine_ref[...], inner_ref[...]
    coefs = [coef_ref[pl.ds(s, 1), :] for s in range(snaps)]
    rows = kinds * zl
    for m in range(kinds):
        for z in range(zl):
            value = jnp.zeros((xl, width), jnp.float32)
            for s in range(snaps):
                at = s * rows + m * zl + z
                value = value + mine[:, at : at + 1] * coefs[s]
            sketch_ref[m, z] = value
    put_sketch = pltpu.make_async_copy(sketch_ref, sketch_hbm, sems.at[0])
    put_sketch.start()
    weighted = jnp.zeros((snaps, width), jnp.float32)
    for s in range(snaps):
        weighted = weighted + inner[:, s : s + 1] * coefs[s]
    stack = coef_ref[...]
    if padding:
        stack = jnp.concatenate([stack, jnp.zeros((padding, width), jnp.float32)], axis=0)
        weighted = jnp.concatenate([weighted, jnp.zeros((padding, width), jnp.float32)], axis=0)
    total_rows = kinds * (xl * snaps) * zl * planes
    gram_ref[...] = jnp.dot(
        stack.T, weighted * (1.0 / total_rows), precision=HIGHEST,
        preferred_element_type=jnp.float32,
    )
    put_gram = pltpu.make_async_copy(gram_ref, gram_hbm, sems.at[1])
    put_gram.start()
    put_sketch.wait()
    put_gram.wait()


def per_device(
    velocity, plane_count, inv_span, kernels, omega_block, omega_table, omega_stream, wall_shear
):
    snaps, planes = lax.axis_size("snap"), lax.axis_size("plane")
    _, slots, comps, zw, xw = velocity.shape
    zf, xf = zw // POOL, xw // POOL
    width = omega_stream.shape[1]
    _, kinds, zs, _ = wall_shear.shape
    zl = zs // POOL
    everyone = snaps * planes <= 64
    receivers = (snaps * planes if everyone else planes) - 1
    vmem = pl.BlockSpec(memory_space=pltpu.VMEM)
    hbm = pl.BlockSpec(memory_space=pltpu.HBM)
    dma = pltpu.SemaphoreType.DMA
    f32, bf16 = jnp.float32, jnp.bfloat16
    stencils = kernels.transpose(0, 2, 1, 3)
    coef, mine, inner = pl.pallas_call(
        functools.partial(kernel, snaps, planes, everyone),
        out_shape=(
            jax.ShapeDtypeStruct((snaps, width), f32),
            jax.ShapeDtypeStruct((xf // snaps, xw), f32),
            jax.ShapeDtypeStruct((snaps, xw), f32),
        ),
        in_specs=[pl.BlockSpec(memory_space=pltpu.SMEM)] + [hbm] * 7,
        out_specs=(vmem, vmem, vmem),
        scratch_shapes=[
            pltpu.SMEM(inv_span.shape, f32),
            pltpu.SMEM(stencils.shape, f32),
            pltpu.SMEM(omega_block.shape, jnp.int32),
            pltpu.VMEM(wall_shear.shape, bf16),
            pltpu.VMEM(omega_stream.shape, bf16),
            pltpu.VMEM((slots, comps, zw, xw), bf16),
            pltpu.VMEM(omega_table.shape, bf16),
            pltpu.VMEM((2 * xw - xf, width), bf16),
            pltpu.VMEM((slots, zf, xw), f32),
            pltpu.VMEM((slots * comps * zw, xw), f32),
            pltpu.VMEM((slots, 2 * comps * zf, xw), bf16),
            pltpu.VMEM((kinds * zs, xw), f32),
            pltpu.VMEM((snaps, kinds * zl, xw), f32),
            pltpu.VMEM((xw, xw), f32),
            pltpu.VMEM((planes, snaps, xw), f32),
            pltpu.VMEM((2, zf, xw), f32),
            pltpu.VMEM((2, zf, xw), f32),
            pltpu.VMEM((snaps * planes, 1, width), f32),
            pltpu.VMEM((snaps, 1, width), f32),
            dma((7,)),
            dma((snaps - 1,)), dma((snaps - 1,)),
            dma((planes - 1,)), dma((planes - 1,)),
            dma((2,)), dma((2,)),
            dma((1 if everyone else receivers,)), dma((1 if everyone else receivers,)),
            dma((snaps - 1,)), dma((snaps - 1,)),
        ],
        compiler_params=pltpu.CompilerParams(
            collective_id=0, has_side_effects=True, vmem_limit_bytes=24 * 1024 * 1024
        ),
    )(
        plane_count,
        *(
            pltpu.with_memory_space_constraint(value, pltpu.HBM)
            for value in (
                inv_span, stencils, omega_block, wall_shear, omega_stream, velocity, omega_table
            )
        )
    )
    sketch_shape = (kinds, zl, xf // snaps, width)
    return pl.pallas_call(
        functools.partial(outputs_kernel, planes),
        out_shape=(pltpu.HBM(sketch_shape, f32), pltpu.HBM((width, width), f32)),
        in_specs=[vmem] * 3,
        out_specs=(hbm, hbm),
        scratch_shapes=[
            pltpu.VMEM(sketch_shape, f32), pltpu.VMEM((width, width), f32), dma((2,)),
        ],
        compiler_params=pltpu.CompilerParams(vmem_limit_bytes=16 * 1024 * 1024),
    )(coef, mine, inner)


def solution(mesh):
    return jax.shard_map(
        per_device,
        mesh=mesh,
        in_specs=(
            P("snap", "plane", None, None, None),
            P("plane"),
            P("plane", None),
            P(),
            P("plane", None),
            P(),
            P(),
            P("snap", None, "plane", None),
        ),
        out_specs=(P(None, "plane", "snap", None), P()),
        check_vma=False,
    )
```
